1024 devices in a mesh: tm: 32 (over z, core), row: 4 (over x), col: 8 (over y).
Axes of the slice: x: 4, y: 8, z: 16, core: 2. Of those that a mesh axis runs over, the one named last changes fastest.
Arguments:
- factor_inverse: bfloat16 [131072, 4096], P(('tm', 'row'), 'col'), as said below
- coupling: bfloat16 [131072, 384], P(('tm', 'col')), as said below
- arrow_block: float32 [384, 384], replicated, as said below
Outputs:
- regression_map: float32 [131072, 384], P(('tm', 'col'))
- arrow_covariance: float32 [384, 384], replicated
Inputs may be any that keep to these rules, and one draw needn't show every extreme that they name: `factor_inverse`: each block of 4096 rows is lower triangular with diagonal entries between 0.5 and 1.5. `coupling`: entries of order one. Symmetric; the whole precision matrix made of the blocks, the coupling and arrow_block is positive definite.
All inputs are finite; a program needn't handle non-finite values.
Results may differ from the reference program's by a relative error of at most 0.0003.
The reference program's roundings to bfloat16 on the way (of `weights`) count: a program that leaves them out, or rounds other values in their place, can miss the bound.
Values may be sent and summed in bfloat16 or wider, within the bound.
No kernel may reach another device: no remote copies, remote signals or barrier semaphores. Data moves between devices by JAX's collectives and lax.ppermute only.
A program may use at most 32 MiB of HBM per device.

```python
import math
import jax
import jax.numpy as jnp
from jax import lax

B = 4096
NA = 384
N_TM = 32


def draw_factor_inverse(key, part):
    key = jax.random.fold_in(key, 11)
    first_key, second_key = jax.random.split(key, 2)
    shape = (N_TM * B, B)
    row_index = lax.broadcasted_iota(jnp.int32, shape, 0) % B
    col_index = lax.broadcasted_iota(jnp.int32, shape, 1)
    diagonal = jnp.exp(jax.random.uniform(first_key, shape, jnp.float32, math.log(0.5), math.log(1.5)))
    lower = jax.random.normal(second_key, shape, jnp.float32) * (0.5 / math.sqrt(B))
    values = jnp.where(row_index == col_index, diagonal, jnp.where(col_index < row_index, lower, 0.0))
    return values.astype(jnp.bfloat16)


def draw_coupling(key, part):
    key = jax.random.fold_in(key, 37)
    second_key = jax.random.fold_in(key, 1)
    shape = (N_TM * B, NA)
    values = jnp.clip(jax.random.normal(second_key, shape, jnp.float32), -6.0, 6.0)
    return values.astype(jnp.bfloat16)


def draw_arrow_block(key, part):
    key = jax.random.fold_in(key, 23)
    first_key, second_key = jax.random.split(key, 2)
    random_part = jax.random.normal(second_key, (NA, NA), jnp.float32)
    symmetric = (random_part + random_part.T) * (0.3 / math.sqrt(2.0 * NA))
    diagonal = jax.random.uniform(first_key, (NA,), jnp.float32, 3.0, 5.0)
    values = (symmetric + jnp.diag(diagonal)) * (N_TM * B)
    return values.astype(jnp.float32)


def setup_inputs(seed: int = 0) -> dict:
    streams_of = jax.random.split(jax.random.key(seed), 4)
    return {
        "factor_inverse": draw_factor_inverse(jax.random.fold_in(streams_of[3], 71), 0),
        "coupling": draw_coupling(jax.random.fold_in(streams_of[3], 71), 0),
        "arrow_block": draw_arrow_block(jax.random.fold_in(streams_of[3], 71), 0),
    }


def gram_pair(block_inverse, coupled):
    weights = jnp.dot(block_inverse.astype(jnp.float32), coupled.astype(jnp.float32), preferred_element_type=jnp.float32).astype(jnp.bfloat16)
    gram = lax.dot_general(weights.astype(jnp.float32), weights.astype(jnp.float32), (((0,), (0,)), ((), ())), preferred_element_type=jnp.float32)
    mapped = lax.dot_general(block_inverse.astype(jnp.float32), weights.astype(jnp.float32), (((0,), (0,)), ((), ())), preferred_element_type=jnp.float32)
    return (gram, mapped)

def covariance(scaled):
    factor = jnp.linalg.cholesky(scaled)
    identity = jnp.eye(scaled.shape[0], dtype=scaled.dtype)
    solved = lax.linalg.triangular_solve(factor, identity, left_side=True, lower=True)
    return jnp.dot(solved.T, solved, precision=lax.Precision.HIGHEST)

def reference(factor_inverse, coupling, arrow_block):

    def per_block(block_index):
        first_row = (block_index * B).astype(jnp.int32)
        block_inverse = lax.dynamic_slice_in_dim(factor_inverse, first_row, B, 0)
        coupled = lax.dynamic_slice_in_dim(coupling, first_row, B, 0)
        return gram_pair(block_inverse, coupled)
    grams, mapped = lax.map(per_block, jnp.arange(N_TM, dtype=jnp.int32))
    gram_total = jnp.sum(grams, axis=0)
    rows_total = N_TM * B
    scaled = (arrow_block - gram_total) / rows_total
    return (-mapped.reshape(rows_total, NA), covariance(scaled))
```

```python
import jax
import jax.numpy as jnp
from jax import lax
from jax.sharding import Mesh, PartitionSpec as P

B = 4096
PLANE = ("core", "row", "col")


def covariance(scaled):
    factor = jnp.linalg.cholesky(scaled)
    identity = jnp.eye(scaled.shape[0], dtype=scaled.dtype)
    solved = lax.linalg.triangular_solve(factor, identity, left_side=True, lower=True)
    return jnp.dot(solved.T, solved, precision=lax.Precision.HIGHEST)


def spread(x, axes):
    copies = jnp.broadcast_to(x[None], (lax.axis_size(axes),) + x.shape)
    return lax.all_to_all(copies, axes, 0, 0, tiled=True)


def pack(gram):
    n = gram.shape[0] // 3
    return jnp.concatenate(
        [gram[:n], jnp.concatenate([gram[n : 2 * n, n:], gram[2 * n :, 2 * n :]], axis=1)]
    )


def unpack(packed):
    n = packed.shape[0] // 2
    a, b, c = (packed[:n, i * n : (i + 1) * n] for i in range(3))
    d, e, f = (packed[n:, i * n : (i + 1) * n] for i in range(3))
    return jnp.block([[a, b, c], [b.T, d, e], [c.T, e.T, f]])


def gram_sum(local_gram):
    plane = lax.axis_size(("core", "row"))
    cols = lax.axis_size("col")
    packed = pack(local_gram)
    rows, width = packed.shape
    piece = rows // (plane * cols)
    mine = lax.dynamic_index_in_dim(
        packed.reshape(plane, cols, piece, width), lax.axis_index("col"), 1, keepdims=False
    )
    part = jnp.sum(lax.all_to_all(mine, ("core", "row"), 0, 0, tiled=True), axis=0)
    total = jnp.sum(spread(part, "z"), axis=0)
    return unpack(spread(total, PLANE).reshape(rows, width))


def per_device(factor_inverse, coupling, arrow_block):
    share = lax.psum_scatter(
        jnp.dot(factor_inverse, coupling, preferred_element_type=jnp.float32),
        "col",
        scatter_dimension=0,
        tiled=True,
    )
    gathered = spread(share.astype(jnp.bfloat16), "col")
    gathered = gathered.reshape(-1, gathered.shape[-1])
    contract = (((0,), (0,)), ((), ()))
    mapped_part = lax.dot_general(
        factor_inverse, gathered, contract, preferred_element_type=jnp.float32
    )
    mapped = lax.psum(mapped_part, "row")
    local_gram = lax.dot_general(
        gathered, gathered, contract, preferred_element_type=jnp.float32
    )
    gram_total = gram_sum(local_gram)
    rows_total = lax.axis_size("z") * lax.axis_size("core") * B
    scaled = (arrow_block - gram_total) / rows_total
    return (-mapped, covariance(scaled))


def solution(mesh):
    tm, row, col = mesh.devices.shape
    split = Mesh(mesh.devices.reshape(tm // 2, 2, row, col), ("z",) + PLANE)
    blocks = P(("z", "core", "col"), None)
    return jax.shard_map(
        per_device,
        mesh=split,
        in_specs=(P(("z", "core", "row"), "col"), blocks, P()),
        out_specs=(blocks, P()),
        check_vma=False,
    )
```

```python
import functools

import jax
import jax.numpy as jnp
from jax import lax
from jax.experimental import pallas as pl
from jax.experimental.pallas import tpu as pltpu
from jax.sharding import Mesh, PartitionSpec as P

B = 4096
PLANE = ("core", "row", "col")


PANEL = 8


def dot32(a, b, left=1, right=0):
    return lax.dot_general(
        a,
        b,
        (((left,), (right,)), ((), ())),
        precision=lax.Precision.HIGHEST,
        preferred_element_type=jnp.float32,
    )


def block_inverse(m):
    n, w = m.shape[0], PANEL
    lane = lax.broadcasted_iota(jnp.int32, (n, n), 1)
    panel_lane = lax.broadcasted_iota(jnp.int32, (w, n), 1)
    sub = lax.broadcasted_iota(jnp.int32, (w, n), 0)
    for k in range(0, n, w):
        rows = m[k : k + w, :]
        cols = [jnp.broadcast_to(rows[:, k + j : k + j + 1], (w, n)) for j in range(w)]
        inside = (panel_lane >= k) & (panel_lane < k + w)
        t = jnp.where(inside, jnp.where(panel_lane == sub + k, 1.0, 0.0), rows)
        for j in range(w):
            inv = 1.0 / cols[j][j : j + 1, :]
            pivot = t[j : j + 1, :] * inv
            t = jnp.where(sub == j, pivot, t - cols[j] * pivot)
            for i in range(j + 1, w):
                p = cols[i][j : j + 1, :] * inv
                cols[i] = jnp.where(sub == j, p, cols[i] - cols[j] * p)
        new = jnp.where((lane >= k) & (lane < k + w), 0.0, m)
        for j in range(w):
            new = new - m[:, k + j : k + j + 1] * t[j : j + 1, :]
        m = jnp.concatenate([x for x in (new[:k], t, new[k + w :]) if x.shape[0]])
    return m


def upper_blocks(products):
    return products[0], jnp.concatenate(products[1:], axis=1)


def weights_kernel(share_ref, copies_ref, pieces_ref):
    weights = share_ref[...].astype(jnp.bfloat16)
    for i in range(copies_ref.shape[0]):
        copies_ref[i] = -weights
    n = weights.shape[1] // 3
    contract = (((0,), (0,)), ((), ()))
    half = pieces_ref.shape[0] // 2
    piece = pieces_ref.shape[1]
    products = [
        lax.dot_general(
            weights[:, i * n : (i + 1) * n],
            weights[:, i * n :],
            contract,
            preferred_element_type=jnp.float32,
        )
        for i in range(3)
    ]
    for upper, block_row in enumerate(upper_blocks(products)):
        for i in range(half):
            pieces_ref[upper * half + i] = block_row[i * piece : (i + 1) * piece]


def sum_kernel(parts_ref, after_ref, copies_ref):
    del after_ref
    total = parts_ref[0]
    for i in range(1, parts_ref.shape[0]):
        total = total + parts_ref[i]
    for i in range(copies_ref.shape[0]):
        copies_ref[i] = total


def inverse_kernel(scale, pieces_ref, arrow_ref, after_ref, out_ref):
    del after_ref
    n = arrow_ref.shape[0] // 3
    half = pieces_ref.shape[0] // 2
    s = [slice(i * n, (i + 1) * n) for i in range(3)]

    def block(i, j):
        first, c = (0, j) if i == 0 else (half, i + j - 2)
        gram = jnp.concatenate([pieces_ref[first + p, :, s[c]] for p in range(half)])
        return (arrow_ref[s[i], s[j]] - gram) * scale

    p0 = block_inverse(block(0, 0))
    a0 = jnp.concatenate([block(0, 1), block(0, 2)], axis=1)
    t0 = dot32(p0, a0)
    low = dot32(a0, t0, 0, 0)
    p1 = block_inverse(block(1, 1) - low[:n, :n])
    a1 = block(1, 2) - low[:n, n:]
    t1 = dot32(p1, a1)
    p2 = block_inverse(block(2, 2) - low[n:, n:] - dot32(a1, t1, 0, 0))
    x12 = -dot32(t1, p2)
    x11 = p1 - dot32(x12, t1, 1, 1)
    rest = jnp.concatenate(
        [jnp.concatenate([x11, x12], axis=1), jnp.concatenate([x12.T, p2], axis=1)]
    )
    x0 = -dot32(t0, rest)
    out_ref[s[0], s[0]] = p0 - dot32(x0, t0, 1, 1)
    out_ref[s[0], n:] = x0
    out_ref[n:, s[0]] = x0.T
    out_ref[n:, n:] = rest


VMEM = pl.BlockSpec(memory_space=pltpu.VMEM)
LATER = pl.BlockSpec(memory_space=pl.ANY)


def call(kernel, out_shape, in_specs, flops):
    return pl.pallas_call(
        kernel,
        out_shape=out_shape,
        in_specs=in_specs,
        out_specs=jax.tree.map(lambda _: VMEM, out_shape),
        compiler_params=pltpu.CompilerParams(vmem_limit_bytes=16 * 2**20),
        cost_estimate=pl.CostEstimate(flops=flops, bytes_accessed=2**20, transcendentals=0),
    )


def exchange(pieces, axes):
    return lax.all_to_all(pieces, axes, 0, 0, tiled=True)


def per_device(factor_inverse, coupling, arrow_block):
    f32 = jnp.float32
    share = lax.psum_scatter(
        jnp.dot(factor_inverse, coupling, preferred_element_type=f32),
        "col",
        scatter_dimension=0,
        tiled=True,
    )
    cols, planes, size = (lax.axis_size(a) for a in ("col", "z", PLANE))
    width = share.shape[1]
    piece = (2 * width // 3 // size, width)
    copies, pieces = call(
        weights_kernel,
        (
            jax.ShapeDtypeStruct((cols,) + share.shape, jnp.bfloat16),
            jax.ShapeDtypeStruct((size,) + piece, f32),
        ),
        [VMEM],
        10**9,
    )(share)
    parts = exchange(pieces, PLANE)
    gathered = exchange(copies, "col").reshape(-1, width)

    mapped_part = lax.dot_general(
        factor_inverse, gathered, (((0,), (0,)), ((), ())), preferred_element_type=f32
    )
    mapped_share = lax.psum_scatter(mapped_part, "row", scatter_dimension=0, tiled=True)
    rows = lax.axis_size("row")
    mapped = exchange(
        jnp.broadcast_to(mapped_share[None], (rows,) + mapped_share.shape), "row"
    ).reshape(-1, width)

    by_plane = call(
        sum_kernel, jax.ShapeDtypeStruct((planes,) + piece, f32), [VMEM, LATER], 10**7
    )(parts, copies)
    by_plane = exchange(by_plane, "z")
    totals = call(
        sum_kernel, jax.ShapeDtypeStruct((size,) + piece, f32), [VMEM, LATER], 10**7
    )(by_plane, mapped_part)
    totals = exchange(totals, PLANE)
    rows_total = planes * lax.axis_size("core") * B
    covariance = call(
        functools.partial(inverse_kernel, 1.0 / rows_total),
        jax.ShapeDtypeStruct(arrow_block.shape, f32),
        [VMEM, VMEM, LATER],
        15 * 10**9,
    )(totals, arrow_block, mapped_share)
    return (mapped, covariance)


def solution(mesh):
    tm, row, col = mesh.devices.shape
    split = Mesh(mesh.devices.reshape(tm // 2, 2, row, col), ("z",) + PLANE)
    blocks = P(("z", "core", "col"), None)
    return jax.shard_map(
        per_device,
        mesh=split,
        in_specs=(P(("z", "core", "row"), "col"), blocks, P()),
        out_specs=(blocks, P()),
        check_vma=False,
    )
```

```python
import functools

import jax
import jax.numpy as jnp
from jax import lax
from jax.experimental import pallas as pl
from jax.experimental.pallas import tpu as pltpu
from jax.sharding import Mesh, PartitionSpec as P

B = 4096
PLANE = ("row", "col")


PANEL = 8


def dot32(a, b, left=1, right=0):
    return lax.dot_general(
        a,
        b,
        (((left,), (right,)), ((), ())),
        precision=lax.Precision.HIGHEST,
        preferred_element_type=jnp.float32,
    )


def block_inverse(m):
    n, w = m.shape[0], PANEL
    lane = lax.broadcasted_iota(jnp.int32, (n, n), 1)
    panel_lane = lax.broadcasted_iota(jnp.int32, (w, n), 1)
    sub = lax.broadcasted_iota(jnp.int32, (w, n), 0)
    for k in range(0, n, w):
        rows = m[k : k + w, :]
        cols = [jnp.broadcast_to(rows[:, k + j : k + j + 1], (w, n)) for j in range(w)]
        inside = (panel_lane >= k) & (panel_lane < k + w)
        t = jnp.where(inside, jnp.where(panel_lane == sub + k, 1.0, 0.0), rows)
        for j in range(w):
            inv = 1.0 / cols[j][j : j + 1, :]
            pivot = t[j : j + 1, :] * inv
            t = jnp.where(sub == j, pivot, t - cols[j] * pivot)
            for i in range(j + 1, w):
                p = cols[i][j : j + 1, :] * inv
                cols[i] = jnp.where(sub == j, p, cols[i] - cols[j] * p)
        new = jnp.where((lane >= k) & (lane < k + w), 0.0, m)
        for j in range(w):
            new = new - m[:, k + j : k + j + 1] * t[j : j + 1, :]
        m = jnp.concatenate([x for x in (new[:k], t, new[k + w :]) if x.shape[0]])
    return m


def gram_kernel(mine_ref, other_ref, pieces_ref):
    weights = jnp.concatenate([mine_ref[...], other_ref[...]])
    n = weights.shape[1] // 3
    piece = pieces_ref.shape[1]

    def product(i):
        return lax.dot_general(
            weights[:, i * n : (i + 1) * n],
            weights[:, i * n :],
            (((0,), (0,)), ((), ())),
            preferred_element_type=jnp.float32,
        )

    def store(block_row):
        for i in range(pieces_ref.shape[0]):
            pieces_ref[i] = block_row[i * piece : (i + 1) * piece]

    core = lax.axis_index("core")

    @pl.when(core == 0)
    def _():
        store(product(0))

    @pl.when(core == 1)
    def _():
        store(jnp.concatenate([product(1), product(2)], axis=1))


def map_kernel(factor_ref, sums_ref, after_ref, out_ref):
    del after_ref
    out_ref[...] = lax.dot_general(
        factor_ref[...],
        -sums_ref[...].astype(jnp.bfloat16),
        (((0,), (0,)), ((), ())),
        preferred_element_type=jnp.float32,
    )


def sum_kernel(parts_ref, after_ref, copies_ref):
    del after_ref
    total = parts_ref[0]
    for i in range(1, parts_ref.shape[0]):
        total = total + parts_ref[i]
    for i in range(copies_ref.shape[0]):
        copies_ref[i] = total


def inverse_kernel(scale, mine_ref, other_ref, arrow_ref, after_ref, out_ref):
    del after_ref
    n = arrow_ref.shape[0] // 3
    s = [slice(i * n, (i + 1) * n) for i in range(3)]
    first = lax.axis_index("core") == 0
    pieces = range(mine_ref.shape[0])

    def block(i, j):
        c = s[j if i == 0 else i + j - 2]
        mine = jnp.concatenate([mine_ref[p, :, c] for p in pieces])
        other = jnp.concatenate([other_ref[p, :, c] for p in pieces])
        gram = jnp.where(first == (i == 0), mine, other)
        return (arrow_ref[s[i], s[j]] - gram) * scale

    p0 = block_inverse(block(0, 0))
    a0 = jnp.concatenate([block(0, 1), block(0, 2)], axis=1)
    t0 = dot32(p0, a0)
    low = dot32(a0, t0, 0, 0)
    p1 = block_inverse(block(1, 1) - low[:n, :n])
    a1 = block(1, 2) - low[:n, n:]
    t1 = dot32(p1, a1)
    p2 = block_inverse(block(2, 2) - low[n:, n:] - dot32(a1, t1, 0, 0))
    x12 = -dot32(t1, p2)
    x11 = p1 - dot32(x12, t1, 1, 1)
    rest = jnp.concatenate(
        [jnp.concatenate([x11, x12], axis=1), jnp.concatenate([x12.T, p2], axis=1)]
    )
    x0 = -dot32(t0, rest)
    out_ref[s[0], s[0]] = p0 - dot32(x0, t0, 1, 1)
    out_ref[s[0], n:] = x0
    out_ref[n:, s[0]] = x0.T
    out_ref[n:, n:] = rest


VMEM = pl.BlockSpec(memory_space=pltpu.VMEM)
LATER = pl.BlockSpec(memory_space=pl.ANY)


def call(kernel, out_shape, in_specs, flops):
    return pl.pallas_call(
        kernel,
        out_shape=out_shape,
        in_specs=in_specs,
        out_specs=jax.tree.map(lambda _: VMEM, out_shape),
        compiler_params=pltpu.CompilerParams(vmem_limit_bytes=16 * 2**20),
        cost_estimate=pl.CostEstimate(flops=flops, bytes_accessed=2**20, transcendentals=0),
    )


def exchange(pieces, axes):
    return lax.all_to_all(pieces, axes, 0, 0, tiled=True)


def swap(x):
    return lax.ppermute(x, "core", [(0, 1), (1, 0)])


def per_device(factor_inverse, coupling, arrow_block):
    f32 = jnp.float32
    shape = jax.ShapeDtypeStruct
    share = lax.psum_scatter(
        jnp.dot(factor_inverse, coupling, preferred_element_type=f32),
        "col",
        scatter_dimension=0,
        tiled=True,
    )
    gathered = lax.all_gather(share, "col", tiled=True)
    weights = share.astype(jnp.bfloat16)
    planes, size, rows = (lax.axis_size(a) for a in ("z", PLANE, "row"))
    width = share.shape[1]
    piece = (width // 3 // size, width)

    pieces = call(gram_kernel, shape((size,) + piece, f32), [VMEM] * 2, 10**9)(
        weights, swap(weights)
    )
    parts = exchange(pieces, PLANE)
    parts = call(sum_kernel, shape((planes,) + piece, f32), [VMEM, LATER], 10**7)(parts, weights)
    parts = exchange(parts, "z")
    mapped_part = call(
        map_kernel,
        shape((factor_inverse.shape[1], width), f32),
        [VMEM, VMEM, LATER],
        10**9,
    )(factor_inverse, gathered, parts)
    mapped_share = lax.psum_scatter(mapped_part, "row", scatter_dimension=0, tiled=True)
    totals = call(sum_kernel, shape((size,) + piece, f32), [VMEM, LATER], 10**7)(
        parts, mapped_part
    )
    totals = exchange(totals, PLANE)
    halves = swap(totals)

    copies = call(sum_kernel, shape((rows,) + mapped_share.shape, f32), [VMEM, LATER], 10**7)(
        mapped_share[None], totals
    )
    mapped = exchange(copies, "row").reshape(-1, width)
    rows_total = planes * lax.axis_size("core") * B
    covariance = call(
        functools.partial(inverse_kernel, 1.0 / rows_total),
        shape(arrow_block.shape, f32),
        [VMEM, VMEM, VMEM, LATER],
        15 * 10**9,
    )(totals, halves, arrow_block, copies)
    return (mapped, covariance)


def solution(mesh):
    tm, row, col = mesh.devices.shape
    split = Mesh(mesh.devices.reshape(tm // 2, 2, row, col), ("z", "core") + PLANE)
    blocks = P(("z", "core", "col"), None)
    return jax.shard_map(
        per_device,
        mesh=split,
        in_specs=(P(("z", "core", "row"), "col"), blocks, P()),
        out_specs=(blocks, P()),
        check_vma=False,
    )
```

```python
import functools

import jax
import jax.numpy as jnp
from jax import lax
from jax.experimental import pallas as pl
from jax.experimental.pallas import tpu as pltpu
from jax.sharding import Mesh, PartitionSpec as P

B = 4096
PLANE = ("row", "col")


PANEL = 8


def dot32(a, b, left=1, right=0):
    return lax.dot_general(
        a,
        b,
        (((left,), (right,)), ((), ())),
        precision=lax.Precision.HIGHEST,
        preferred_element_type=jnp.float32,
    )


def block_inverse(m):
    n, w = m.shape[0], PANEL
    lane = lax.broadcasted_iota(jnp.int32, (n, n), 1)
    panel_lane = lax.broadcasted_iota(jnp.int32, (w, n), 1)
    sub = lax.broadcasted_iota(jnp.int32, (w, n), 0)
    for k in range(0, n, w):
        rows = m[k : k + w, :]
        cols = [jnp.broadcast_to(rows[:, k + j : k + j + 1], (w, n)) for j in range(w)]
        inside = (panel_lane >= k) & (panel_lane < k + w)
        t = jnp.where(inside, jnp.where(panel_lane == sub + k, 1.0, 0.0), rows)
        for j in range(w):
            inv = 1.0 / cols[j][j : j + 1, :]
            pivot = t[j : j + 1, :] * inv
            t = jnp.where(sub == j, pivot, t - cols[j] * pivot)
            for i in range(j + 1, w):
                p = cols[i][j : j + 1, :] * inv
                cols[i] = jnp.where(sub == j, p, cols[i] - cols[j] * p)
        new = jnp.where((lane >= k) & (lane < k + w), 0.0, m)
        for j in range(w):
            new = new - m[:, k + j : k + j + 1] * t[j : j + 1, :]
        m = jnp.concatenate([x for x in (new[:k], t, new[k + w :]) if x.shape[0]])
    return m


def gram_kernel(mine_ref, other_ref, pieces_ref):
    weights = jnp.concatenate([mine_ref[...], other_ref[...]])
    n = weights.shape[1] // 3
    piece = pieces_ref.shape[1]

    def product(i):
        return lax.dot_general(
            weights[:, i * n : (i + 1) * n],
            weights[:, i * n :],
            (((0,), (0,)), ((), ())),
            preferred_element_type=jnp.float32,
        )

    def store(block_row):
        for i in range(pieces_ref.shape[0]):
            pieces_ref[i] = block_row[i * piece : (i + 1) * piece]

    core = lax.axis_index("core")

    @pl.when(core == 0)
    def _():
        store(product(0))

    @pl.when(core == 1)
    def _():
        store(jnp.concatenate([product(1), product(2)], axis=1))


def turned(axis, distance):
    n = lax.axis_size(axis)
    steps = jnp.where(lax.axis_index("core") == 0, distance % n, -distance % n)
    return lax.rem(lax.axis_index(axis) + steps, n)


def chunk(axis, distance, size):
    return pl.ds(pl.multiple_of(turned(axis, distance) * size, size), size)


def join_kernel(parts_ref, second_ref, first_ref, copies_ref, pair_ref):
    fan_out(sum_of(parts_ref), copies_ref)
    n = first_ref.shape[0]
    pair_ref[:n] = second_ref[...]
    pair_ref[n:] = first_ref[...]


def map_kernel(factor_ref, *refs):
    *rows_refs, _ = refs[:8]
    *out_refs, weights_ref = refs[8:]
    distance = -4
    n = rows_refs[-1].shape[0]
    for ref in rows_refs:
        for i in range(ref.shape[0] // n):
            weights_ref[chunk("col", distance, n), :] = ref[i * n : (i + 1) * n]
            distance += 1
    for distance, out_ref in enumerate(out_refs):
        out_ref[...] = -lax.dot_general(
            factor_ref[:, chunk("row", distance, out_ref.shape[0])],
            weights_ref[...],
            (((0,), (0,)), ((), ())),
            preferred_element_type=jnp.float32,
        )


def sum_of(ref):
    total = ref[0]
    for i in range(1, ref.shape[0]):
        total = total + ref[i]
    return total


def fan_out(x, copies_ref):
    for i in range(copies_ref.shape[0]):
        copies_ref[i] = x


def sum_kernel(parts_ref, after_ref, copies_ref):
    del after_ref
    fan_out(sum_of(parts_ref), copies_ref)


def add_kernel(a_ref, b_ref, c_ref, d_ref, after_ref, copies_ref):
    del after_ref
    fan_out((a_ref[...] + b_ref[...]) + (c_ref[...] + d_ref[...]), copies_ref)


def inverse_kernel(scale, mine_ref, other_ref, arrow_ref, after_ref, out_ref):
    del after_ref
    n = arrow_ref.shape[0] // 3
    s = [slice(i * n, (i + 1) * n) for i in range(3)]
    first = lax.axis_index("core") == 0
    pieces = range(mine_ref.shape[0])

    def block(i, j):
        c = s[j if i == 0 else i + j - 2]
        mine = jnp.concatenate([mine_ref[p, :, c] for p in pieces])
        other = jnp.concatenate([other_ref[p, :, c] for p in pieces])
        gram = jnp.where(first == (i == 0), mine, other)
        return (arrow_ref[s[i], s[j]] - gram) * scale

    p0 = block_inverse(block(0, 0))
    a0 = jnp.concatenate([block(0, 1), block(0, 2)], axis=1)
    t0 = dot32(p0, a0)
    low = dot32(a0, t0, 0, 0)
    p1 = block_inverse(block(1, 1) - low[:n, :n])
    a1 = block(1, 2) - low[:n, n:]
    t1 = dot32(p1, a1)
    p2 = block_inverse(block(2, 2) - low[n:, n:] - dot32(a1, t1, 0, 0))
    x12 = -dot32(t1, p2)
    x11 = p1 - dot32(x12, t1, 1, 1)
    rest = jnp.concatenate(
        [jnp.concatenate([x11, x12], axis=1), jnp.concatenate([x12.T, p2], axis=1)]
    )
    x0 = -dot32(t0, rest)
    out_ref[s[0], s[0]] = p0 - dot32(x0, t0, 1, 1)
    out_ref[s[0], n:] = x0
    out_ref[n:, s[0]] = x0.T
    out_ref[n:, n:] = rest


VMEM = pl.BlockSpec(memory_space=pltpu.VMEM)
LATER = pl.BlockSpec(memory_space=pl.ANY)


def call(kernel, out_shape, in_specs, flops, scratch=()):
    return pl.pallas_call(
        kernel,
        out_shape=out_shape,
        in_specs=in_specs,
        out_specs=jax.tree.map(lambda _: VMEM, out_shape),
        scratch_shapes=scratch,
        compiler_params=pltpu.CompilerParams(vmem_limit_bytes=16 * 2**20),
        cost_estimate=pl.CostEstimate(flops=flops, bytes_accessed=2**20, transcendentals=0),
    )


def exchange(pieces, axes):
    return lax.all_to_all(pieces, axes, 0, 0, tiled=True)


def shift(x, axis, distance):
    n = lax.axis_size(axis)
    ways = ((0, distance), (n, -distance))
    return lax.ppermute(
        x,
        ("core", axis),
        [(first + i, first + (i + d) % n) for first, d in ways for i in range(n)],
    )


def swap(x):
    return lax.ppermute(x, "core", [(0, 1), (1, 0)])


def far_kernel(factor_ref, coupling_ref, up_ref, down_ref):
    half, n = up_ref.shape[0], 2 * up_ref.shape[0]
    far = jnp.dot(
        factor_ref[chunk("col", 4, n), :], coupling_ref[...], preferred_element_type=jnp.float32
    )
    up_ref[...] = far[:half]
    down_ref[...] = far[half:]


def near_kernel(factor_ref, coupling_ref, after_ref, *out_refs):
    del after_ref
    for i, out_ref in enumerate(out_refs):
        out_ref[...] = jnp.dot(
            factor_ref[chunk("col", i - 3, out_ref.shape[0]), :],
            coupling_ref[...],
            preferred_element_type=jnp.float32,
        )


def first_kernel(ahead_ref, behind_ref, up_ref, down_ref, ahead_out, behind_out):
    half = up_ref.shape[0]
    ahead_out[:half] = ahead_ref[:half] + up_ref[...]
    ahead_out[half:] = ahead_ref[half:]
    behind_out[:half] = behind_ref[:half]
    behind_out[half:] = behind_ref[half:] + down_ref[...]


def step_kernel(ahead_ref, behind_ref, up_ref, down_ref, ahead_out, behind_out):
    ahead_out[...] = ahead_ref[...] + up_ref[...]
    behind_out[...] = behind_ref[...] + down_ref[...]


def last_kernel(mine_ref, up_ref, down_ref, out_ref):
    out_ref[...] = (mine_ref[...] + (up_ref[...] + down_ref[...])).astype(out_ref.dtype)


def ring_weights(factor_inverse, coupling):
    shape = jax.ShapeDtypeStruct
    rows = factor_inverse.shape[0] // lax.axis_size("col")
    width = coupling.shape[1]
    full = shape((rows, width), jnp.float32)
    half = shape((rows // 2, width), jnp.float32)
    far = call(far_kernel, (half,) * 2, [VMEM] * 2, 10**8)(factor_inverse, coupling)
    near = call(near_kernel, (full,) * 7, [VMEM, VMEM, LATER], 10**9)(
        factor_inverse, coupling, far[0]
    )
    up, down = far
    for distance in (3, 2, 1):
        up, down = shift(up, "col", 1), shift(down, "col", -1)
        up, down = call(
            first_kernel if distance == 3 else step_kernel, (full,) * 2, [VMEM] * 4, 10**7
        )(near[3 + distance], near[3 - distance], up, down)
    up, down = shift(up, "col", 1), shift(down, "col", -1)
    return call(last_kernel, shape(full.shape, jnp.bfloat16), [VMEM] * 3, 10**7)(
        near[3], up, down
    )


def per_device(factor_inverse, coupling, arrow_block):
    f32 = jnp.float32
    shape = jax.ShapeDtypeStruct
    weights = ring_weights(factor_inverse, coupling)
    planes, size, rows, cols = (lax.axis_size(a) for a in ("z", PLANE, "row", "col"))
    height, width = weights.shape
    piece = (width // 3 // size, width)

    other = swap(weights)
    near = {d: shift(weights, "col", -d) for d in (-1, 1, -2, 2)}
    pieces = call(gram_kernel, shape((size,) + piece, f32), [VMEM] * 2, 10**9)(weights, other)
    parts = exchange(pieces, PLANE)
    parts, pair = call(
        join_kernel,
        (shape((planes,) + piece, f32), shape((2 * height, width), weights.dtype)),
        [VMEM] * 3,
        10**7,
    )(parts, near[-2], near[-1])
    far = shift(pair, "col", 2), shift(near[1], "col", -2)
    parts = exchange(parts, "z")
    block = shape((factor_inverse.shape[1] // rows, width), f32)
    mapped = call(
        map_kernel,
        (block,) * rows,
        [VMEM] * 8 + [LATER],
        10**9,
        [pltpu.VMEM((cols * height, width), weights.dtype)],
    )(factor_inverse, far[0], near[-2], near[-1], weights, near[1], near[2], far[1], parts)
    arrived = [shift(mapped[d], "row", d) for d in range(1, rows)]
    totals = call(sum_kernel, shape((size,) + piece, f32), [VMEM, LATER], 10**7)(
        parts, mapped[0]
    )
    totals = exchange(totals, PLANE)
    halves = swap(totals)
    copies = call(add_kernel, shape((rows,) + block.shape, f32), [VMEM] * 4 + [LATER], 10**7)(
        mapped[0], *arrived, totals
    )
    mapped = exchange(copies, "row").reshape(-1, width)
    rows_total = planes * lax.axis_size("core") * B
    covariance = call(
        functools.partial(inverse_kernel, 1.0 / rows_total),
        shape(arrow_block.shape, f32),
        [VMEM, VMEM, VMEM, LATER],
        15 * 10**9,
    )(totals, halves, arrow_block, copies)
    return (mapped, covariance)


def solution(mesh):
    tm, row, col = mesh.devices.shape
    split = Mesh(mesh.devices.reshape(tm // 2, 2, row, col), ("z", "core") + PLANE)
    blocks = P(("z", "core", "col"), None)
    return jax.shard_map(
        per_device,
        mesh=split,
        in_specs=(P(("z", "core", "row"), "col"), blocks, P()),
        out_specs=(blocks, P()),
        check_vma=False,
    )
```

```python
import functools

import jax
import jax.numpy as jnp
from jax import lax
from jax.experimental import pallas as pl
from jax.experimental.pallas import tpu as pltpu
from jax.sharding import Mesh, PartitionSpec as P

B = 4096
PLANE = ("row", "col")


PANEL = 8


def dot32(a, b, left=1, right=0):
    return lax.dot_general(
        a,
        b,
        (((left,), (right,)), ((), ())),
        precision=lax.Precision.HIGHEST,
        preferred_element_type=jnp.float32,
    )


def block_inverse(m):
    n, w = m.shape[0], PANEL
    lane = lax.broadcasted_iota(jnp.int32, (n, n), 1)
    panel_lane = lax.broadcasted_iota(jnp.int32, (w, n), 1)
    sub = lax.broadcasted_iota(jnp.int32, (w, n), 0)
    for k in range(0, n, w):
        rows = m[k : k + w, :]
        cols = [jnp.broadcast_to(rows[:, k + j : k + j + 1], (w, n)) for j in range(w)]
        inside = (panel_lane >= k) & (panel_lane < k + w)
        t = jnp.where(inside, jnp.where(panel_lane == sub + k, 1.0, 0.0), rows)
        for j in range(w):
            inv = 1.0 / cols[j][j : j + 1, :]
            pivot = t[j : j + 1, :] * inv
            t = jnp.where(sub == j, pivot, t - cols[j] * pivot)
            for i in range(j + 1, w):
                p = cols[i][j : j + 1, :] * inv
                cols[i] = jnp.where(sub == j, p, cols[i] - cols[j] * p)
        new = jnp.where((lane >= k) & (lane < k + w), 0.0, m)
        for j in range(w):
            new = new - m[:, k + j : k + j + 1] * t[j : j + 1, :]
        m = jnp.concatenate([x for x in (new[:k], t, new[k + w :]) if x.shape[0]])
    return m


def gram_kernel(mine_ref, other_ref, pieces_ref):
    weights = jnp.concatenate([mine_ref[...], other_ref[...]])
    n = weights.shape[1] // 3
    count, piece = pieces_ref.shape[0] // 2, pieces_ref.shape[1]
    upper = [
        lax.dot_general(
            weights[:, i * n : (i + 1) * n],
            weights[:, i * n :],
            (((0,), (0,)), ((), ())),
            preferred_element_type=jnp.float32,
        )
        for i in range(3)
    ]
    for row, block_row in enumerate((upper[0], jnp.concatenate(upper[1:], axis=1))):
        for i in range(count):
            pieces_ref[row * count + i] = block_row[i * piece : (i + 1) * piece]


def turned(axis, distance):
    n = lax.axis_size(axis)
    steps = jnp.where(lax.axis_index("core") == 0, distance % n, -distance % n)
    return lax.rem(lax.axis_index(axis) + steps, n)


def chunk(axis, distance, size):
    return pl.ds(pl.multiple_of(turned(axis, distance) * size, size), size)


def pair_kernel(mine_ref, other_ref, copies_ref):
    fan_out(jnp.concatenate([other_ref[...], mine_ref[...]]), copies_ref)


def map_kernel(mine_ref, other_ref, gathered_ref, out_ref, weights_ref):
    n = gathered_ref.shape[1] // 2
    m = out_ref.shape[1] // 2
    for part, factor_ref in enumerate((other_ref, mine_ref)):
        for i in range(gathered_ref.shape[0]):
            weights_ref[i * n : (i + 1) * n] = gathered_ref[i, part * n : (part + 1) * n]
        for i in range(out_ref.shape[0]):
            out_ref[i, part * m : (part + 1) * m] = -lax.dot_general(
                factor_ref[:, i * m : (i + 1) * m],
                weights_ref[...],
                (((0,), (0,)), ((), ())),
                preferred_element_type=jnp.float32,
            )


def part_kernel(both_ref, mine_ref, other_ref):
    m = both_ref.shape[1] // 2
    for i in range(both_ref.shape[0]):
        other_ref[i * m : (i + 1) * m] = both_ref[i, :m]
        mine_ref[i * m : (i + 1) * m] = both_ref[i, m:]


def sum_of(ref):
    total = ref[0]
    for i in range(1, ref.shape[0]):
        total = total + ref[i]
    return total


def fan_out(x, copies_ref):
    for i in range(copies_ref.shape[0]):
        copies_ref[i] = x


def sum_kernel(parts_ref, copies_ref):
    fan_out(sum_of(parts_ref), copies_ref)


def inverse_kernel(scale, packed_ref, arrow_ref, out_ref, spare_ref):
    size = arrow_ref.shape[0]
    n = size // 3
    s = [slice(i * n, (i + 1) * n) for i in range(3)]

    def block(i, j):
        gram = packed_ref[s[0], s[j]] if i == 0 else packed_ref[s[1], s[i + j - 2]]
        return (arrow_ref[s[i], s[j]] - gram) * scale

    p0 = block_inverse(block(0, 0))
    a0 = jnp.concatenate([block(0, 1), block(0, 2)], axis=1)
    t0 = dot32(p0, a0)
    low = dot32(a0, t0, 0, 0)
    p1 = block_inverse(block(1, 1) - low[:n, :n])
    a1 = block(1, 2) - low[:n, n:]
    t1 = dot32(p1, a1)
    p2 = block_inverse(block(2, 2) - low[n:, n:] - dot32(a1, t1, 0, 0))
    x12 = -dot32(t1, p2)
    x11 = p1 - dot32(x12, t1, 1, 1)
    rest = jnp.concatenate(
        [jnp.concatenate([x11, x12], axis=1), jnp.concatenate([x12.T, p2], axis=1)]
    )
    x0 = -dot32(t0, rest)
    out_ref[s[0], s[0]] = p0 - dot32(x0, t0, 1, 1)
    out_ref[s[0], n:] = x0
    out_ref[n:size, s[0]] = x0.T
    out_ref[n:size, n:] = rest
    out_ref[size:] = jnp.zeros_like(out_ref[size:])
    spare_ref[...] = jnp.zeros_like(spare_ref)


VMEM = pl.BlockSpec(memory_space=pltpu.VMEM)
LATER = pl.BlockSpec(memory_space=pl.ANY)


def call(kernel, out_shape, in_specs, flops, scratch=()):
    return pl.pallas_call(
        kernel,
        out_shape=out_shape,
        in_specs=in_specs,
        out_specs=jax.tree.map(lambda _: VMEM, out_shape),
        scratch_shapes=scratch,
        compiler_params=pltpu.CompilerParams(vmem_limit_bytes=16 * 2**20),
        cost_estimate=pl.CostEstimate(flops=flops, bytes_accessed=2**20, transcendentals=0),
    )


def exchange(pieces, axes):
    return lax.all_to_all(pieces, axes, 0, 0, tiled=True)


def shift(x, axis, distance):
    n = lax.axis_size(axis)
    ways = ((0, distance), (n, -distance))
    return lax.ppermute(
        x,
        ("core", axis),
        [(first + i, first + (i + d) % n) for first, d in ways for i in range(n)],
    )


def swap(x):
    return lax.ppermute(x, "core", [(0, 1), (1, 0)])


def ring_rows(distance, rows):
    return turned("col", distance) * rows


def far_kernel(*refs):
    factors, couplings, (half_ref, third_ref) = refs[:2], refs[2:4], refs[4:6]
    rows_ref, nodes_ref, ready = refs[6:]
    part_rows, rows = half_ref.shape[1], third_ref.shape[1]
    half = ring_rows(4, rows) + lax.axis_index("core") * part_rows
    copies = []
    for part in range(2):
        for source, target in (
            (factors[part].at[pl.ds(pl.multiple_of(half, part_rows), part_rows), :],
             rows_ref.at[part, pl.ds(0, part_rows), :]),
            (factors[part].at[pl.ds(pl.multiple_of(ring_rows(3, rows), rows), rows), :],
             rows_ref.at[part, pl.ds(part_rows, rows), :]),
            (couplings[part], nodes_ref.at[part]),
        ):
            copies.append(pltpu.make_async_copy(source, target, ready.at[len(copies)]))
    for copy in copies:
        copy.start()
    for copy in copies:
        copy.wait()
    for part in range(2):
        products = jnp.dot(
            rows_ref[part], nodes_ref[part], preferred_element_type=jnp.float32
        )
        half_ref[part] = products[:part_rows]
        third_ref[part] = products[part_rows:]


def near_kernel(*refs):
    factors, couplings, out_refs = refs[:2], refs[2:4], refs[5:]
    for distance, out_ref in zip((1, 2, 0), out_refs):
        rows = out_ref.shape[1]
        first = pl.multiple_of(ring_rows(distance, rows), rows)
        for part in range(2):
            out_ref[part] = jnp.dot(
                factors[part][pl.ds(first, rows), :],
                couplings[part][...],
                preferred_element_type=jnp.float32,
            )


def merge_kernel(second_ref, third_ref, half_ref, out_ref):
    out_ref[...] = second_ref[...] + third_ref[...]
    size = half_ref.shape[1]
    rows = pl.ds(pl.multiple_of(lax.axis_index("core") * size, size), size)
    for part in range(half_ref.shape[0]):
        out_ref[part, rows, :] = out_ref[part, rows, :] + half_ref[part]


def add_kernel(a_ref, b_ref, out_ref):
    out_ref[...] = a_ref[...] + b_ref[...]


def last_kernel(own_ref, mine_ref, received_ref, weights_ref, other_ref):
    for part, out_ref in enumerate((weights_ref, other_ref)):
        total = own_ref[part] + (mine_ref[part] + received_ref[1 - part])
        out_ref[...] = total.astype(out_ref.dtype)


def ring_weights(factors, couplings):
    shape = jax.ShapeDtypeStruct
    rows = factors[0].shape[0] // lax.axis_size("col")
    width = couplings[0].shape[1]
    full = shape((2, rows, width), jnp.float32)
    operands = (*factors, *couplings)
    nodes, dtype = factors[0].shape[1], factors[0].dtype
    half, third = call(
        far_kernel,
        (shape((2, rows // 2, width), jnp.float32), full),
        [LATER] * 4,
        10**8,
        [
            pltpu.VMEM((2, 3 * rows // 2, nodes), dtype),
            pltpu.VMEM((2, nodes, width), dtype),
            pltpu.SemaphoreType.DMA((6,)),
        ],
    )(*operands)
    after, second, own = call(near_kernel, (full,) * 3, [VMEM] * 4 + [LATER], 10**8)(
        *operands, half
    )
    half, third = shift(half, "col", 2), shift(third, "col", 1)
    second = call(merge_kernel, full, [VMEM] * 3, 10**7)(second, third, half)
    total = call(add_kernel, full, [VMEM] * 2, 10**7)(
        shift(after, "col", 1), shift(second, "col", 2)
    )
    weights = shape((rows, width), jnp.bfloat16)
    return call(last_kernel, (weights,) * 2, [VMEM] * 3, 10**7)(own, total, swap(total))


def covariance_branch(weights, other, factor, other_factor, arrow_block):
    del other_factor
    f32 = jnp.float32
    shape = jax.ShapeDtypeStruct
    planes, size = lax.axis_size("z"), lax.axis_size(PLANE)
    width = weights.shape[1]
    piece = (2 * width // 3 // size, width)
    parts = call(gram_kernel, shape((size,) + piece, f32), [VMEM] * 2, 10**9)(weights, other)
    parts = exchange(parts, PLANE)
    parts = call(sum_kernel, shape((planes,) + piece, f32), [VMEM], 10**7)(parts)
    parts = exchange(parts, "z")
    parts = call(sum_kernel, shape((size,) + piece, f32), [VMEM], 10**7)(parts)
    packed = exchange(parts, PLANE).reshape(-1, width)
    covariance, spare = call(
        functools.partial(inverse_kernel, 1.0 / (planes * lax.axis_size("core") * B)),
        (shape((factor.shape[1], width), f32),) * 2,
        [VMEM] * 2,
        15 * 10**9,
    )(packed, arrow_block)
    return spare, covariance


def map_branch(weights, other, factor, other_factor, arrow_block):
    del arrow_block
    f32 = jnp.float32
    shape = jax.ShapeDtypeStruct
    cols, rows = lax.axis_size("col"), lax.axis_size("row")
    height, width = weights.shape
    copies = call(
        pair_kernel, shape((cols, 2 * height, width), weights.dtype), [VMEM] * 2, 10**7
    )(weights, other)
    gathered = exchange(copies, "col")
    both = shape((rows, 2 * factor.shape[1] // rows, width), f32)
    parts = call(
        map_kernel,
        both,
        [VMEM] * 3,
        2 * 10**9,
        [pltpu.VMEM((cols * height, width), weights.dtype)],
    )(factor, other_factor, gathered)
    copies = call(sum_kernel, both, [VMEM], 10**7)(exchange(parts, "row"))
    maps = exchange(copies, "row")
    return call(part_kernel, (shape((factor.shape[1], width), f32),) * 2, [VMEM], 10**7)(maps)


def per_device(factor_inverse, coupling, arrow_block):
    other_factor = swap(factor_inverse)
    weights, other = ring_weights((factor_inverse, other_factor), (coupling, swap(coupling)))
    mine, sent = lax.cond(
        lax.axis_index("core") == 0,
        covariance_branch,
        map_branch,
        weights,
        other,
        factor_inverse,
        other_factor,
        arrow_block,
    )
    received = swap(sent)
    first = lax.axis_index("core") == 0
    rows = arrow_block.shape[0]
    return (
        jnp.where(first, received, mine),
        jnp.where(first, sent[:rows], received[:rows]),
    )


def solution(mesh):
    tm, row, col = mesh.devices.shape
    split = Mesh(mesh.devices.reshape(tm // 2, 2, row, col), ("z", "core") + PLANE)
    blocks = P(("z", "core", "col"), None)
    return jax.shard_map(
        per_device,
        mesh=split,
        in_specs=(P(("z", "core", "row"), "col"), blocks, P()),
        out_specs=(blocks, P()),
        check_vma=False,
    )
```

```python
import functools

import jax
import jax.numpy as jnp
from jax import lax
from jax.experimental import pallas as pl
from jax.experimental.pallas import tpu as pltpu
from jax.sharding import Mesh, PartitionSpec as P

B = 4096
PLANE = ("row", "col")


PANEL = 8


def dot32(a, b, left=1, right=0):
    return lax.dot_general(
        a,
        b,
        (((left,), (right,)), ((), ())),
        precision=lax.Precision.HIGHEST,
        preferred_element_type=jnp.float32,
    )


def block_inverse(m):
    n, w = m.shape[0], PANEL
    lane = lax.broadcasted_iota(jnp.int32, (n, n), 1)
    panel_lane = lax.broadcasted_iota(jnp.int32, (w, n), 1)
    sub = lax.broadcasted_iota(jnp.int32, (w, n), 0)
    for k in range(0, n, w):
        rows = m[k : k + w, :]
        cols = [jnp.broadcast_to(rows[:, k + j : k + j + 1], (w, n)) for j in range(w)]
        inside = (panel_lane >= k) & (panel_lane < k + w)
        t = jnp.where(inside, jnp.where(panel_lane == sub + k, 1.0, 0.0), rows)
        for j in range(w):
            inv = 1.0 / cols[j][j : j + 1, :]
            pivot = t[j : j + 1, :] * inv
            t = jnp.where(sub == j, pivot, t - cols[j] * pivot)
            for i in range(j + 1, w):
                p = cols[i][j : j + 1, :] * inv
                cols[i] = jnp.where(sub == j, p, cols[i] - cols[j] * p)
        new = jnp.where((lane >= k) & (lane < k + w), 0.0, m)
        for j in range(w):
            new = new - m[:, k + j : k + j + 1] * t[j : j + 1, :]
        m = jnp.concatenate([x for x in (new[:k], t, new[k + w :]) if x.shape[0]])
    return m


def gram_kernel(mine_ref, other_ref, pieces_ref):
    weights = jnp.concatenate([mine_ref[...], other_ref[...]])
    n = weights.shape[1] // 3
    count, piece = pieces_ref.shape[0] // 2, pieces_ref.shape[1]
    upper = [
        lax.dot_general(
            weights[:, i * n : (i + 1) * n],
            weights[:, i * n :],
            (((0,), (0,)), ((), ())),
            preferred_element_type=jnp.float32,
        )
        for i in range(3)
    ]
    for row, block_row in enumerate((upper[0], jnp.concatenate(upper[1:], axis=1))):
        for i in range(count):
            pieces_ref[row * count + i] = block_row[i * piece : (i + 1) * piece]


def turned(axis, distance):
    n = lax.axis_size(axis)
    steps = jnp.where(lax.axis_index("core") == 0, distance % n, -distance % n)
    return lax.rem(lax.axis_index(axis) + steps, n)


def chunk(axis, distance, size):
    return pl.ds(pl.multiple_of(turned(axis, distance) * size, size), size)


def pair_kernel(first, mine_ref, other_ref, after_ref, copies_ref):
    del after_ref
    rows = slice(first, first + copies_ref.shape[1] // 2)
    fan_out(jnp.concatenate([other_ref[rows], mine_ref[rows]]), copies_ref)


def map_kernel(mine_ref, other_ref, few_ref, many_ref, out_ref, weights_ref):
    m = out_ref.shape[1] // 2
    for part, factor_ref in enumerate((other_ref, mine_ref)):
        first = 0
        for i in range(few_ref.shape[0]):
            for ref in (few_ref, many_ref):
                n = ref.shape[1] // 2
                weights_ref[first : first + n] = ref[i, part * n : (part + 1) * n]
                first += n
        for i in range(out_ref.shape[0]):
            out_ref[i, part * m : (part + 1) * m] = -lax.dot_general(
                factor_ref[:, i * m : (i + 1) * m],
                weights_ref[...],
                (((0,), (0,)), ((), ())),
                preferred_element_type=jnp.float32,
            )


def part_kernel(both_ref, mine_ref, other_ref):
    m = both_ref.shape[1] // 2
    for i in range(both_ref.shape[0]):
        other_ref[i * m : (i + 1) * m] = both_ref[i, :m]
        mine_ref[i * m : (i + 1) * m] = both_ref[i, m:]


def sum_of(ref):
    total = ref[0]
    for i in range(1, ref.shape[0]):
        total = total + ref[i]
    return total


def fan_out(x, copies_ref):
    for i in range(copies_ref.shape[0]):
        copies_ref[i] = x


def sum_kernel(parts_ref, copies_ref):
    fan_out(sum_of(parts_ref), copies_ref)


def inverse_kernel(scale, packed_ref, arrow_ref, out_ref, spare_ref):
    size = arrow_ref.shape[0]
    n = size // 3
    s = [slice(i * n, (i + 1) * n) for i in range(3)]

    def block(i, j):
        gram = packed_ref[s[0], s[j]] if i == 0 else packed_ref[s[1], s[i + j - 2]]
        return (arrow_ref[s[i], s[j]] - gram) * scale

    p0 = block_inverse(block(0, 0))
    a0 = jnp.concatenate([block(0, 1), block(0, 2)], axis=1)
    t0 = dot32(p0, a0)
    low = dot32(a0, t0, 0, 0)
    p1 = block_inverse(block(1, 1) - low[:n, :n])
    a1 = block(1, 2) - low[:n, n:]
    t1 = dot32(p1, a1)
    p2 = block_inverse(block(2, 2) - low[n:, n:] - dot32(a1, t1, 0, 0))
    x12 = -dot32(t1, p2)
    x11 = p1 - dot32(x12, t1, 1, 1)
    rest = jnp.concatenate(
        [jnp.concatenate([x11, x12], axis=1), jnp.concatenate([x12.T, p2], axis=1)]
    )
    x0 = -dot32(t0, rest)
    out_ref[s[0], s[0]] = p0 - dot32(x0, t0, 1, 1)
    out_ref[s[0], n:] = x0
    out_ref[n:size, s[0]] = x0.T
    out_ref[n:size, n:] = rest
    out_ref[size:] = jnp.zeros_like(out_ref[size:])
    spare_ref[...] = jnp.zeros_like(spare_ref)


VMEM = pl.BlockSpec(memory_space=pltpu.VMEM)
LATER = pl.BlockSpec(memory_space=pl.ANY)


def call(kernel, out_shape, in_specs, flops, scratch=()):
    return pl.pallas_call(
        kernel,
        out_shape=out_shape,
        in_specs=in_specs,
        out_specs=jax.tree.map(lambda _: VMEM, out_shape),
        scratch_shapes=scratch,
        compiler_params=pltpu.CompilerParams(vmem_limit_bytes=16 * 2**20),
        cost_estimate=pl.CostEstimate(flops=flops, bytes_accessed=2**20, transcendentals=0),
    )


def exchange(pieces, axes):
    return lax.all_to_all(pieces, axes, 0, 0, tiled=True)


def shift(x, axis, distance):
    n = lax.axis_size(axis)
    ways = ((0, distance), (n, -distance))
    return lax.ppermute(
        x,
        ("core", axis),
        [(first + i, first + (i + d) % n) for first, d in ways for i in range(n)],
    )


def swap(x):
    return lax.ppermute(x, "core", [(0, 1), (1, 0)])


def ring_rows(distance, rows):
    return turned("col", distance) * rows


def far_kernel(*refs):
    factors, couplings, (half_ref, third_ref) = refs[:2], refs[2:4], refs[4:6]
    rows_ref, nodes_ref, ready = refs[6:]
    part_rows, rows = half_ref.shape[1], third_ref.shape[1]
    half = ring_rows(4, rows) + lax.axis_index("core") * part_rows
    copies = []
    for part in range(2):
        for source, target in (
            (factors[part].at[pl.ds(pl.multiple_of(half, part_rows), part_rows), :],
             rows_ref.at[part, pl.ds(0, part_rows), :]),
            (factors[part].at[pl.ds(pl.multiple_of(ring_rows(3, rows), rows), rows), :],
             rows_ref.at[part, pl.ds(part_rows, rows), :]),
            (couplings[part], nodes_ref.at[part]),
        ):
            copies.append(pltpu.make_async_copy(source, target, ready.at[len(copies)]))
    for copy in copies:
        copy.start()
    for copy in copies:
        copy.wait()
    for part in range(2):
        products = jnp.dot(
            rows_ref[part], nodes_ref[part], preferred_element_type=jnp.float32
        )
        half_ref[part] = products[:part_rows]
        third_ref[part] = products[part_rows:]


def near_kernel(*refs):
    factors, couplings, out_refs = refs[:2], refs[2:4], refs[5:]
    for distance, out_ref in zip((1, 2, 0), out_refs):
        rows = out_ref.shape[1]
        first = pl.multiple_of(ring_rows(distance, rows), rows)
        for part in range(2):
            out_ref[part] = jnp.dot(
                factors[part][pl.ds(first, rows), :],
                couplings[part][...],
                preferred_element_type=jnp.float32,
            )


def merge_kernel(second_ref, third_ref, half_ref, out_ref):
    out_ref[...] = second_ref[...] + third_ref[...]
    size = half_ref.shape[1]
    rows = pl.ds(pl.multiple_of(lax.axis_index("core") * size, size), size)
    for part in range(half_ref.shape[0]):
        out_ref[part, rows, :] = out_ref[part, rows, :] + half_ref[part]


def add_kernel(a_ref, b_ref, out_ref):
    out_ref[...] = a_ref[...] + b_ref[...]


def last_kernel(own_ref, mine_ref, received_ref, weights_ref, other_ref):
    for part, out_ref in enumerate((weights_ref, other_ref)):
        total = own_ref[part] + (mine_ref[part] + received_ref[1 - part])
        out_ref[...] = total.astype(out_ref.dtype)


def ring_weights(factors, couplings):
    shape = jax.ShapeDtypeStruct
    rows = factors[0].shape[0] // lax.axis_size("col")
    width = couplings[0].shape[1]
    full = shape((2, rows, width), jnp.float32)
    operands = (*factors, *couplings)
    nodes, dtype = factors[0].shape[1], factors[0].dtype
    half, third = call(
        far_kernel,
        (shape((2, rows // 2, width), jnp.float32), full),
        [LATER] * 4,
        10**8,
        [
            pltpu.VMEM((2, 3 * rows // 2, nodes), dtype),
            pltpu.VMEM((2, nodes, width), dtype),
            pltpu.SemaphoreType.DMA((6,)),
        ],
    )(*operands)
    after, second, own = call(near_kernel, (full,) * 3, [VMEM] * 4 + [LATER], 10**8)(
        *operands, half
    )
    half, third = shift(half, "col", 2), shift(third, "col", 1)
    second = call(merge_kernel, full, [VMEM] * 3, 10**7)(second, third, half)
    total = call(add_kernel, full, [VMEM] * 2, 10**7)(
        shift(after, "col", 1), shift(second, "col", 2)
    )
    weights = shape((rows, width), jnp.bfloat16)
    return call(last_kernel, (weights,) * 2, [VMEM] * 3, 10**7)(own, total, swap(total))


def covariance_branch(weights, other, factor, other_factor, arrow_block):
    del other_factor
    f32 = jnp.float32
    shape = jax.ShapeDtypeStruct
    planes, size = lax.axis_size("z"), lax.axis_size(PLANE)
    width = weights.shape[1]
    piece = (2 * width // 3 // size, width)
    parts = call(gram_kernel, shape((size,) + piece, f32), [VMEM] * 2, 10**9)(weights, other)
    parts = exchange(parts, PLANE)
    parts = call(sum_kernel, shape((planes,) + piece, f32), [VMEM], 10**7)(parts)
    parts = exchange(parts, "z")
    parts = call(sum_kernel, shape((size,) + piece, f32), [VMEM], 10**7)(parts)
    packed = exchange(parts, PLANE).reshape(-1, width)
    covariance, spare = call(
        functools.partial(inverse_kernel, 1.0 / (planes * lax.axis_size("core") * B)),
        (shape((factor.shape[1], width), f32),) * 2,
        [VMEM] * 2,
        15 * 10**9,
    )(packed, arrow_block)
    return spare, covariance


def map_branch(weights, other, factor, other_factor, arrow_block):
    del arrow_block
    f32 = jnp.float32
    shape = jax.ShapeDtypeStruct
    cols, rows = lax.axis_size("col"), lax.axis_size("row")
    height, width = weights.shape

    def gather(first, count, after):
        copies = call(
            functools.partial(pair_kernel, first),
            shape((cols, 2 * count, width), weights.dtype),
            [VMEM, VMEM, LATER],
            10**7,
        )(weights, other, after)
        return exchange(copies, "col")

    few = gather(0, height // 4, weights)
    many = gather(height // 4, height - height // 4, few)
    both = shape((rows, 2 * factor.shape[1] // rows, width), f32)
    parts = call(
        map_kernel,
        both,
        [VMEM] * 4,
        2 * 10**9,
        [pltpu.VMEM((cols * height, width), weights.dtype)],
    )(factor, other_factor, few, many)
    copies = call(sum_kernel, both, [VMEM], 10**7)(exchange(parts, "row"))
    maps = exchange(copies, "row")
    return call(part_kernel, (shape((factor.shape[1], width), f32),) * 2, [VMEM], 10**7)(maps)


def per_device(factor_inverse, coupling, arrow_block):
    other_factor = swap(factor_inverse)
    weights, other = ring_weights((factor_inverse, other_factor), (coupling, swap(coupling)))
    mine, sent = lax.cond(
        lax.axis_index("core") == 0,
        covariance_branch,
        map_branch,
        weights,
        other,
        factor_inverse,
        other_factor,
        arrow_block,
    )
    received = swap(sent)
    first = lax.axis_index("core") == 0
    rows = arrow_block.shape[0]
    return (
        jnp.where(first, received, mine),
        jnp.where(first, sent[:rows], received[:rows]),
    )


def solution(mesh):
    tm, row, col = mesh.devices.shape
    split = Mesh(mesh.devices.reshape(tm // 2, 2, row, col), ("z", "core") + PLANE)
    blocks = P(("z", "core", "col"), None)
    return jax.shard_map(
        per_device,
        mesh=split,
        in_specs=(P(("z", "core", "row"), "col"), blocks, P()),
        out_specs=(blocks, P()),
        check_vma=False,
    )
```

```python
import functools

import jax
import jax.numpy as jnp
from jax import lax
from jax.experimental import pallas as pl
from jax.experimental.pallas import tpu as pltpu
from jax.sharding import Mesh, PartitionSpec as P

B = 4096
PLANE = ("row", "col")


PANEL = 8


def dot32(a, b, left=1, right=0):
    return lax.dot_general(
        a,
        b,
        (((left,), (right,)), ((), ())),
        precision=lax.Precision.HIGHEST,
        preferred_element_type=jnp.float32,
    )


def block_inverse(m):
    n, w = m.shape[0], PANEL
    lane = lax.broadcasted_iota(jnp.int32, (n, n), 1)
    panel_lane = lax.broadcasted_iota(jnp.int32, (w, n), 1)
    sub = lax.broadcasted_iota(jnp.int32, (w, n), 0)
    for k in range(0, n, w):
        rows = m[k : k + w, :]
        cols = [jnp.broadcast_to(rows[:, k + j : k + j + 1], (w, n)) for j in range(w)]
        inside = (panel_lane >= k) & (panel_lane < k + w)
        t = jnp.where(inside, jnp.where(panel_lane == sub + k, 1.0, 0.0), rows)
        for j in range(w):
            inv = 1.0 / cols[j][j : j + 1, :]
            pivot = t[j : j + 1, :] * inv
            t = jnp.where(sub == j, pivot, t - cols[j] * pivot)
            for i in range(j + 1, w):
                p = cols[i][j : j + 1, :] * inv
                cols[i] = jnp.where(sub == j, p, cols[i] - cols[j] * p)
        new = jnp.where((lane >= k) & (lane < k + w), 0.0, m)
        for j in range(w):
            new = new - m[:, k + j : k + j + 1] * t[j : j + 1, :]
        m = jnp.concatenate([x for x in (new[:k], t, new[k + w :]) if x.shape[0]])
    return m


def gram_kernel(mine_ref, other_ref, pieces_ref):
    weights = jnp.concatenate([mine_ref[...], other_ref[...]])
    n = weights.shape[1] // 3
    count, piece = pieces_ref.shape[0] // 2, pieces_ref.shape[1]
    upper = [
        lax.dot_general(
            weights[:, i * n : (i + 1) * n],
            weights[:, i * n :],
            (((0,), (0,)), ((), ())),
            preferred_element_type=jnp.float32,
        )
        for i in range(3)
    ]
    for row, block_row in enumerate((upper[0], jnp.concatenate(upper[1:], axis=1))):
        for i in range(count):
            pieces_ref[row * count + i] = block_row[i * piece : (i + 1) * piece]


def turned(axis, distance):
    n = lax.axis_size(axis)
    steps = jnp.where(lax.axis_index("core") == 0, distance % n, -distance % n)
    return lax.rem(lax.axis_index(axis) + steps, n)


def chunk(axis, distance, size):
    return pl.ds(pl.multiple_of(turned(axis, distance) * size, size), size)


def pair_kernel(first, mine_ref, other_ref, after_ref, copies_ref):
    del after_ref
    rows = slice(first, first + copies_ref.shape[1] // 2)
    fan_out(jnp.concatenate([other_ref[rows], mine_ref[rows]]), copies_ref)


def map_kernel(mine_ref, other_ref, few_ref, many_ref, out_ref, weights_ref):
    m = out_ref.shape[1] // 2
    for part, factor_ref in enumerate((other_ref, mine_ref)):
        first = 0
        for i in range(few_ref.shape[0]):
            for ref in (few_ref, many_ref):
                n = ref.shape[1] // 2
                weights_ref[first : first + n] = ref[i, part * n : (part + 1) * n]
                first += n
        for i in range(out_ref.shape[0]):
            out_ref[i, part * m : (part + 1) * m] = -lax.dot_general(
                factor_ref[:, i * m : (i + 1) * m],
                weights_ref[...],
                (((0,), (0,)), ((), ())),
                preferred_element_type=jnp.float32,
            )


def part_kernel(both_ref, mine_ref, other_ref):
    m = both_ref.shape[1] // 2
    for i in range(both_ref.shape[0]):
        other_ref[i * m : (i + 1) * m] = both_ref[i, :m]
        mine_ref[i * m : (i + 1) * m] = both_ref[i, m:]


def sum_of(ref):
    total = ref[0]
    for i in range(1, ref.shape[0]):
        total = total + ref[i]
    return total


def fan_out(x, copies_ref):
    for i in range(copies_ref.shape[0]):
        copies_ref[i] = x


def sum_kernel(parts_ref, copies_ref):
    fan_out(sum_of(parts_ref), copies_ref)


def inverse_kernel(scale, packed_ref, arrow_ref, out_ref, spare_ref):
    size = arrow_ref.shape[0]
    n = size // 3
    s = [slice(i * n, (i + 1) * n) for i in range(3)]

    def block(i, j):
        gram = packed_ref[s[0], s[j]] if i == 0 else packed_ref[s[1], s[i + j - 2]]
        return (arrow_ref[s[i], s[j]] - gram) * scale

    p0 = block_inverse(block(0, 0))
    a0 = jnp.concatenate([block(0, 1), block(0, 2)], axis=1)
    t0 = dot32(p0, a0)
    low = dot32(a0, t0, 0, 0)
    p1 = block_inverse(block(1, 1) - low[:n, :n])
    a1 = block(1, 2) - low[:n, n:]
    t1 = dot32(p1, a1)
    p2 = block_inverse(block(2, 2) - low[n:, n:] - dot32(a1, t1, 0, 0))
    x12 = -dot32(t1, p2)
    x11 = p1 - dot32(x12, t1, 1, 1)
    rest = jnp.concatenate(
        [jnp.concatenate([x11, x12], axis=1), jnp.concatenate([x12.T, p2], axis=1)]
    )
    x0 = -dot32(t0, rest)
    out_ref[s[0], s[0]] = p0 - dot32(x0, t0, 1, 1)
    out_ref[s[0], n:] = x0
    out_ref[n:size, s[0]] = x0.T
    out_ref[n:size, n:] = rest
    out_ref[size:] = jnp.zeros_like(out_ref[size:])
    spare_ref[...] = jnp.zeros_like(spare_ref)


VMEM = pl.BlockSpec(memory_space=pltpu.VMEM)
LATER = pl.BlockSpec(memory_space=pl.ANY)


def call(kernel, out_shape, in_specs, flops, scratch=()):
    return pl.pallas_call(
        kernel,
        out_shape=out_shape,
        in_specs=in_specs,
        out_specs=jax.tree.map(lambda _: VMEM, out_shape),
        scratch_shapes=scratch,
        compiler_params=pltpu.CompilerParams(vmem_limit_bytes=16 * 2**20),
        cost_estimate=pl.CostEstimate(flops=flops, bytes_accessed=2**20, transcendentals=0),
    )


def exchange(pieces, axes):
    return lax.all_to_all(pieces, axes, 0, 0, tiled=True)


def shift(x, axis, distance):
    n = lax.axis_size(axis)
    ways = ((0, distance), (n, -distance))
    return lax.ppermute(
        x,
        ("core", axis),
        [(first + i, first + (i + d) % n) for first, d in ways for i in range(n)],
    )


def swap(x):
    return lax.ppermute(x, "core", [(0, 1), (1, 0)])


def ring_rows(distance, rows):
    return turned("col", distance) * rows


def far_kernel(*refs):
    factors, couplings, (half_ref, third_ref) = refs[:2], refs[2:4], refs[4:6]
    rows_ref, nodes_ref, ready = refs[6:]
    part_rows, rows = half_ref.shape[1], third_ref.shape[1]
    half = ring_rows(4, rows) + lax.axis_index("core") * part_rows
    copies = []
    for part in range(2):
        for source, target in (
            (factors[part].at[pl.ds(pl.multiple_of(half, part_rows), part_rows), :],
             rows_ref.at[part, pl.ds(0, part_rows), :]),
            (factors[part].at[pl.ds(pl.multiple_of(ring_rows(3, rows), rows), rows), :],
             rows_ref.at[part, pl.ds(part_rows, rows), :]),
            (couplings[part], nodes_ref.at[part]),
        ):
            copies.append(pltpu.make_async_copy(source, target, ready.at[len(copies)]))
    for copy in copies:
        copy.start()
    for copy in copies:
        copy.wait()
    for part in range(2):
        products = jnp.dot(
            rows_ref[part], nodes_ref[part], preferred_element_type=jnp.float32
        )
        half_ref[part] = products[:part_rows]
        third_ref[part] = products[part_rows:]


def near_kernel(*refs):
    factors, couplings, out_refs = refs[:2], refs[2:4], refs[5:]
    for distance, out_ref in zip((1, 2, 0), out_refs):
        rows = out_ref.shape[1]
        first = pl.multiple_of(ring_rows(distance, rows), rows)
        for part in range(2):
            out_ref[part] = jnp.dot(
                factors[part][pl.ds(first, rows), :],
                couplings[part][...],
                preferred_element_type=jnp.float32,
            )


def merge_kernel(second_ref, third_ref, half_ref, out_ref):
    out_ref[...] = second_ref[...] + third_ref[...]
    size = half_ref.shape[1]
    rows = pl.ds(pl.multiple_of(lax.axis_index("core") * size, size), size)
    for part in range(half_ref.shape[0]):
        out_ref[part, rows, :] = out_ref[part, rows, :] + half_ref[part]


def add_kernel(a_ref, b_ref, out_ref):
    out_ref[...] = a_ref[...] + b_ref[...]


def last_kernel(own_ref, mine_ref, received_ref, weights_ref, other_ref):
    for part, out_ref in enumerate((weights_ref, other_ref)):
        total = own_ref[part] + (mine_ref[part] + received_ref[1 - part])
        out_ref[...] = total.astype(out_ref.dtype)


def ring_weights(factors, couplings):
    shape = jax.ShapeDtypeStruct
    rows = factors[0].shape[0] // lax.axis_size("col")
    width = couplings[0].shape[1]
    full = shape((2, rows, width), jnp.float32)
    operands = (*factors, *couplings)
    nodes, dtype = factors[0].shape[1], factors[0].dtype
    half, third = call(
        far_kernel,
        (shape((2, rows // 2, width), jnp.float32), full),
        [LATER] * 4,
        10**8,
        [
            pltpu.VMEM((2, 3 * rows // 2, nodes), dtype),
            pltpu.VMEM((2, nodes, width), dtype),
            pltpu.SemaphoreType.DMA((6,)),
        ],
    )(*operands)
    after, second, own = call(near_kernel, (full,) * 3, [VMEM] * 4 + [LATER], 10**8)(
        *operands, half
    )
    half, third = shift(half, "col", 2), shift(third, "col", 1)
    second = call(merge_kernel, full, [VMEM] * 3, 10**7)(second, third, half)
    total = call(add_kernel, full, [VMEM] * 2, 10**7)(
        shift(after, "col", 1), shift(second, "col", 2)
    )
    weights = shape((rows, width), jnp.bfloat16)
    return call(last_kernel, (weights,) * 2, [VMEM] * 3, 10**7)(own, total, swap(total))


def covariance_branch(weights, other, factor, other_factor, arrow_block):
    del other_factor
    f32 = jnp.float32
    shape = jax.ShapeDtypeStruct
    planes, size = lax.axis_size("z"), lax.axis_size(PLANE)
    width = weights.shape[1]
    piece = (2 * width // 3 // size, width)
    parts = call(gram_kernel, shape((size,) + piece, f32), [VMEM] * 2, 10**9)(weights, other)
    parts = exchange(parts, PLANE)
    parts = call(sum_kernel, shape((planes,) + piece, f32), [VMEM], 10**7)(parts)
    parts = exchange(parts, "z")
    parts = call(sum_kernel, shape((size,) + piece, f32), [VMEM], 10**7)(parts)
    packed = exchange(parts, PLANE).reshape(-1, width)
    covariance, spare = call(
        functools.partial(inverse_kernel, 1.0 / (planes * lax.axis_size("core") * B)),
        (shape((factor.shape[1], width), f32),) * 2,
        [VMEM] * 2,
        15 * 10**9,
    )(packed, arrow_block)
    return spare, covariance


def map_branch(weights, other, factor, other_factor, arrow_block):
    del arrow_block
    f32 = jnp.float32
    shape = jax.ShapeDtypeStruct
    cols, rows = lax.axis_size("col"), lax.axis_size("row")
    height, width = weights.shape

    def gather(first, count, after):
        copies = call(
            functools.partial(pair_kernel, first),
            shape((cols, 2 * count, width), weights.dtype),
            [VMEM, VMEM, LATER],
            10**7,
        )(weights, other, after)
        return exchange(copies, "col")

    few = gather(0, height // 8, weights)
    many = gather(height // 8, height - height // 8, few)
    both = shape((rows, 2 * factor.shape[1] // rows, width), f32)
    parts = call(
        map_kernel,
        both,
        [VMEM] * 4,
        2 * 10**9,
        [pltpu.VMEM((cols * height, width), weights.dtype)],
    )(factor, other_factor, few, many)
    copies = call(sum_kernel, both, [VMEM], 10**7)(exchange(parts, "row"))
    maps = exchange(copies, "row")
    return call(part_kernel, (shape((factor.shape[1], width), f32),) * 2, [VMEM], 10**7)(maps)


def per_device(factor_inverse, coupling, arrow_block):
    other_factor = swap(factor_inverse)
    weights, other = ring_weights((factor_inverse, other_factor), (coupling, swap(coupling)))
    mine, sent = lax.cond(
        lax.axis_index("core") == 0,
        covariance_branch,
        map_branch,
        weights,
        other,
        factor_inverse,
        other_factor,
        arrow_block,
    )
    received = swap(sent)
    first = lax.axis_index("core") == 0
    rows = arrow_block.shape[0]
    return (
        jnp.where(first, received, mine),
        jnp.where(first, sent[:rows], received[:rows]),
    )


def solution(mesh):
    tm, row, col = mesh.devices.shape
    split = Mesh(mesh.devices.reshape(tm // 2, 2, row, col), ("z", "core") + PLANE)
    blocks = P(("z", "core", "col"), None)
    return jax.shard_map(
        per_device,
        mesh=split,
        in_specs=(P(("z", "core", "row"), "col"), blocks, P()),
        out_specs=(blocks, P()),
        check_vma=False,
    )
```
